32 devices in a mesh: dp: 4 (over y, x), space: 8 (over z, core).
Axes of the slice: x: 2, y: 2, z: 4, core: 2. Of those that a mesh axis runs over, the one named last changes fastest.
Arguments:
- volume: bfloat16 [4, 128, 16, 16, 256], P('dp', None, 'space'), may hold values from -6 to 6
- w_first: bfloat16 [3, 3, 3, 128, 256], replicated, may hold values from -0.109375 to 0.109375
- w_second: bfloat16 [3, 3, 3, 256, 512], P(None, None, None, 'space'), may hold values from -0.078125 to 0.078125
- cotangent: bfloat16 [4, 512, 4, 256], P('dp', 'space'), may hold values from -6 to 6
Outputs:
- grad_second: float32 [3, 3, 3, 256, 512], P(None, None, None, 'space')
- pre_grad: bfloat16 [4, 256, 8, 4, 256], P('dp', None, 'space')
The draws below stay inside these ranges and needn't reach their ends.
All inputs are finite; a program needn't handle non-finite values.
Results may differ from the reference program's by a relative error of at most 0.0049.
Values may be sent and summed in bfloat16 or wider, within the bound.
A program may use at most 128 MiB of HBM per device.

```python
import jax
import jax.numpy as jnp
from jax import lax

C1 = 128
C2 = 256
C3 = 512
HGT = 32
WID = 128
SAMPLES = 4
D1 = 16
N_SPACE = 8


def block_levels(own_key, dims, split, smallest, largest):
    def one(axis_at, blocks):
        draws = jax.random.uniform(jax.random.fold_in(jax.random.fold_in(own_key, 6), axis_at), (blocks,), jnp.float32, smallest / len(split), largest / len(split))
        return jnp.repeat(jnp.exp(draws), dims[axis_at] // blocks).reshape((-1,) + (1,) * (len(dims) - axis_at - 1))

    loudness = one(*split[0])
    for cut in split[1:]:
        loudness = loudness * one(*cut)
    return loudness


def centred(own_key, dims, scale, most, pieces=(), held_as=jnp.bfloat16):
    loudness = block_levels(own_key, dims, pieces, -0.22, 0.18) if pieces else 1.0
    entries = jax.random.normal(own_key, dims, jnp.float32) * scale * loudness
    return jnp.minimum(jnp.maximum(entries, -most), most).astype(held_as)


def setup_inputs(seed: int = 0) -> dict:
    seeds = jax.random.split(jax.random.key(seed), 5)
    volume = centred(seeds[0], (SAMPLES, C1, D1, 16, (HGT // 4) * (WID // 4)), 1.0, 6.0, ((0, 4), (2, 8)))
    w_first = centred(seeds[1], (3, 3, 3, C1, C2), (27 * C1) ** -0.5, 0.109375)
    w_second = centred(seeds[2], (3, 3, 3, C2, C3), (27 * C2) ** -0.5, 0.078125, ((3, 8),))
    cotangent = centred(seeds[3], (SAMPLES, C3, D1 // 4, (HGT // 4) * (WID // 4)), 1.0, 6.0, ((0, 4), (1, 8)))
    return {"volume": volume, "w_first": w_first, "w_second": w_second, "cotangent": cotangent}


leak_slope = 0.3

def activate(values):
    return leak_slope * values + (1.0 - leak_slope) * values * jax.nn.sigmoid(values)

def slope_of(values):
    sigmoid_value = jax.nn.sigmoid(values)
    return leak_slope + (1.0 - leak_slope) * (sigmoid_value + values * sigmoid_value * (1.0 - sigmoid_value))

def stride_taps(values, along_dim):
    length = values.shape[along_dim] // 2
    paired = values.reshape(values.shape[:along_dim] + (length, 2) + values.shape[along_dim + 1:])
    even_cells = lax.index_in_dim(paired, 0, along_dim + 1, keepdims=False)
    odd_cells = lax.index_in_dim(paired, 1, along_dim + 1, keepdims=False)
    before = jnp.concatenate([jnp.zeros_like(lax.slice_in_dim(odd_cells, 0, 1, axis=along_dim)), lax.slice_in_dim(odd_cells, 0, length - 1, axis=along_dim)], along_dim)
    return [before, even_cells, odd_cells]

def step_cells(values, by_row, by_col, row_len):
    cells = values.shape[-1]
    if by_row:
        filler = jnp.zeros(values.shape[:-1] + (row_len,), values.dtype)
        values = jnp.concatenate([filler, values[..., :cells - row_len]], -1)
    if by_col:
        filler = jnp.zeros(values.shape[:-1] + (1,), values.dtype)
        moved = jnp.concatenate([filler, values[..., :cells - 1]], -1)
        keeper = lax.iota(jnp.int32, cells) % row_len != 0
        values = jnp.where(keeper, moved, jnp.zeros_like(moved))
    return values

def plane_taps(values, row_len):
    phases = values.shape[-2]
    out_phases = phases // 2
    collected = []
    for row_tap in range(3):
        for col_tap in range(3):
            rows_out = []
            for row_phase in range(out_phases):
                cols_out = []
                for col_phase in range(out_phases):
                    row_at = 2 * row_phase + row_tap - 1
                    col_at = 2 * col_phase + col_tap - 1
                    part = values[..., row_at % phases, col_at % phases, :]
                    cols_out.append(step_cells(part, row_at < 0, col_at < 0, row_len))
                rows_out.append(jnp.stack(cols_out, -2))
            collected.append(jnp.stack(rows_out, -3))
    return collected

def all_taps(values, row_len):
    collected = []
    for depth_part in stride_taps(values, 1):
        collected.extend(plane_taps(depth_part, row_len))
    return collected

def contract_first(left_side, right_side):
    return lax.dot_general(left_side, right_side, (((0,), (0,)), ((), ())), preferred_element_type=jnp.float32)

def contract_last(left_side, right_side):
    return lax.dot_general(left_side, right_side, (((1,), (1,)), ((), ())), preferred_element_type=jnp.float32)

def reference(volume, w_first, w_second, cotangent):
    group_size = C2 // N_SPACE
    row_len = WID // 4
    cell_count = HGT // 4 * (WID // 4)

    def one_sample(inputs):
        volume_one, cot_one = inputs
        volume_cells = volume_one.reshape(C1, D1, 4, 4, cell_count)
        stacked = jnp.stack(all_taps(volume_cells, row_len), 0).reshape(27 * C1, -1)
        pre_act = contract_first(w_first.reshape(27 * C1, C2), stacked)
        hidden = activate(pre_act).astype(jnp.bfloat16).reshape(C2, D1 // 2, 2, 2, cell_count)
        cot_flat = cot_one.reshape(C3, -1)

        def per_group(group_index):
            block_cells = lax.dynamic_slice_in_dim(hidden, group_index * group_size, group_size, 0)
            block_taps = jnp.stack(all_taps(block_cells, row_len), 0).reshape(27 * group_size, -1)
            weight_grad = contract_last(block_taps, cot_flat)
            weight_rows = lax.dynamic_slice_in_dim(w_second, group_index * group_size, group_size, 3).reshape(27 * group_size, C3)
            tap_terms = jnp.dot(weight_rows, cot_flat, preferred_element_type=jnp.float32)

            def spread(field):
                return jnp.stack(all_taps(field, row_len), 0).reshape(27 * group_size, -1)
            unused, pull = jax.vjp(spread, jnp.zeros((group_size, D1 // 2, 2, 2, cell_count), jnp.float32))
            back_terms = pull(tap_terms)[0]
            return (weight_grad, back_terms)
        grad_blocks, back_blocks = lax.map(per_group, jnp.arange(N_SPACE, dtype=jnp.int32))
        grad_full = grad_blocks.reshape(N_SPACE, 3, 3, 3, group_size, C3).transpose(1, 2, 3, 0, 4, 5).reshape(3, 3, 3, C2, C3)
        hidden_grad = back_blocks.reshape(C2, D1 // 2, 4, cell_count).astype(jnp.bfloat16)
        hidden_grad = lax.optimization_barrier(hidden_grad)
        slopes = slope_of(pre_act.reshape(C2, D1 // 2, 4, cell_count))
        result = (hidden_grad.astype(jnp.float32) * slopes).astype(jnp.bfloat16)
        return (grad_full, result)
    grad_samples, pre_grad = lax.map(one_sample, (volume, cotangent))
    grad_second = lax.optimization_barrier(jnp.sum(grad_samples, 0))
    return (grad_second, pre_grad)
```

```python
import functools

import jax
import jax.numpy as jnp
from jax import lax
from jax.experimental import pallas as pl
from jax.experimental.pallas import tpu as pltpu
from jax.sharding import PartitionSpec as P

C3 = 512
WID = 128


leak_slope = 0.3


def from_behind(block, axis, distance):
    devices = range(lax.axis_size(axis))
    route = [(i - distance, i) for i in devices if i - distance in devices]
    return lax.ppermute(block, axis, route)


def activate(values):
    return leak_slope * values + (1.0 - leak_slope) * values * jax.nn.sigmoid(values)


def slope_of(values):
    sigmoid_value = jax.nn.sigmoid(values)
    return leak_slope + (1.0 - leak_slope) * (
        sigmoid_value + values * sigmoid_value * (1.0 - sigmoid_value)
    )


def stride_taps(values, along_dim):
    length = values.shape[along_dim] // 2
    paired = values.reshape(values.shape[:along_dim] + (length, 2) + values.shape[along_dim + 1 :])
    even_cells = lax.index_in_dim(paired, 0, along_dim + 1, keepdims=False)
    odd_cells = lax.index_in_dim(paired, 1, along_dim + 1, keepdims=False)
    before = jnp.concatenate(
        [
            jnp.zeros_like(lax.slice_in_dim(odd_cells, 0, 1, axis=along_dim)),
            lax.slice_in_dim(odd_cells, 0, length - 1, axis=along_dim),
        ],
        along_dim,
    )
    return [before, even_cells, odd_cells]


def step_cells(values, by_row, by_col, row_len):
    cells = values.shape[-1]
    if by_row:
        filler = jnp.zeros(values.shape[:-1] + (row_len,), values.dtype)
        values = jnp.concatenate([filler, values[..., : cells - row_len]], -1)
    if by_col:
        filler = jnp.zeros(values.shape[:-1] + (1,), values.dtype)
        moved = jnp.concatenate([filler, values[..., : cells - 1]], -1)
        keeper = lax.iota(jnp.int32, cells) % row_len != 0
        values = jnp.where(keeper, moved, jnp.zeros_like(moved))
    return values


def plane_taps(values, row_len):
    phases = values.shape[-2]
    out_phases = phases // 2
    collected = []
    for row_tap in range(3):
        for col_tap in range(3):
            rows_out = []
            for row_phase in range(out_phases):
                cols_out = []
                for col_phase in range(out_phases):
                    row_at = 2 * row_phase + row_tap - 1
                    col_at = 2 * col_phase + col_tap - 1
                    part = values[..., row_at % phases, col_at % phases, :]
                    cols_out.append(step_cells(part, row_at < 0, col_at < 0, row_len))
                rows_out.append(jnp.stack(cols_out, -2))
            collected.append(jnp.stack(rows_out, -3))
    return collected


def all_taps(values, row_len):
    collected = []
    for depth_part in stride_taps(values, 1):
        collected.extend(plane_taps(depth_part, row_len))
    return collected


def contract_first(left_side, right_side):
    return lax.dot_general(
        left_side, right_side, (((0,), (0,)), ((), ())), preferred_element_type=jnp.float32
    )


def contract_last(left_side, right_side):
    return lax.dot_general(
        left_side, right_side, (((1,), (1,)), ((), ())), preferred_element_type=jnp.float32
    )


def plain_device(volume, w_first, w_second, cotangent):
    channels = volume.shape[1]
    depth_cells = volume.shape[2]
    cell_count = volume.shape[4]
    half_depth = depth_cells // 2
    out_channels = w_first.shape[4]
    row_len = WID // 4
    paired = volume[0].reshape(channels, half_depth, 2, 4, 4, cell_count)
    even_cells = paired[:, :, 0]
    odd_cells = paired[:, :, 1]
    w_flat = w_first.reshape(27 * channels, out_channels)
    rim_cells = from_behind(odd_cells, "space", 1)
    before = jnp.concatenate([rim_cells, odd_cells[:, : half_depth - 1]], 1)
    collected = []
    for depth_part in (before, even_cells, odd_cells):
        collected.extend(plane_taps(depth_part, row_len))
    stacked = jnp.stack(collected, 0).reshape(27 * channels, -1)
    pre_act = contract_first(w_flat, stacked).reshape(out_channels, half_depth, 4, cell_count)
    hidden = activate(pre_act).astype(jnp.bfloat16)
    by_channel = lax.all_to_all(hidden, "space", split_axis=0, concat_axis=1, tiled=True)
    own_channels = by_channel.shape[0]
    full_depth = by_channel.shape[1]
    hidden_cells = by_channel.reshape(own_channels, full_depth, 2, 2, cell_count)
    hidden_taps = jnp.stack(all_taps(hidden_cells, row_len), 0).reshape(27 * own_channels, -1)
    w_rows = w_second.reshape(27 * own_channels, C3)
    out_cells = hidden_taps.shape[1]
    gathered = lax.all_gather(cotangent[0], "space", axis=0, tiled=True)
    cot_flat = gathered.reshape(C3, out_cells)
    weight_grad = contract_last(hidden_taps, cot_flat)
    tap_terms = jnp.dot(w_rows, cot_flat, preferred_element_type=jnp.float32)
    grad_second = lax.psum(weight_grad, "dp").reshape(3, 3, 3, own_channels, C3)

    def spread(field):
        return jnp.stack(all_taps(field, row_len), 0).reshape(27 * own_channels, -1)

    unused, pull = jax.vjp(
        spread, jnp.zeros((own_channels, full_depth, 2, 2, cell_count), jnp.float32)
    )
    back_terms = pull(tap_terms)[0]
    back_terms = back_terms.astype(jnp.bfloat16).reshape(own_channels, full_depth, 4, cell_count)
    hidden_grad = lax.all_to_all(back_terms, "space", split_axis=1, concat_axis=0, tiled=True)
    pre_grad = (hidden_grad.astype(jnp.float32) * slope_of(pre_act)).astype(jnp.bfloat16)
    return (grad_second, pre_grad[None])


def moved_cells(block, by_row, by_col, row_len):
    if not (by_row or by_col):
        return block
    cells = block.shape[-1]
    at = lax.broadcasted_iota(jnp.int32, block.shape, 1)
    wide = block.astype(jnp.float32)
    if by_row:
        wide = jnp.where(at >= row_len, pltpu.roll(wide, row_len, 1), 0.0)
    if by_col:
        wide = jnp.where(at % row_len != 0, pltpu.roll(wide, 1, 1), 0.0)
    return wide.astype(block.dtype)


def moved_back(block, by_row, by_col, row_len):
    cells = block.shape[-1]
    at = lax.broadcasted_iota(jnp.int32, block.shape, 1)
    if by_row:
        block = pltpu.roll(jnp.where(at >= row_len, block, 0.0), cells - row_len, 1)
    if by_col:
        block = pltpu.roll(jnp.where(at % row_len != 0, block, 0.0), cells - 1, 1)
    return block


def fill_taps(plane, taps, row_len):
    _, channels, cells = plane.shape
    for row_tap in range(3):
        for col_tap in range(3):
            top = (row_tap * 3 + col_tap) * channels
            for row_phase in range(2):
                for col_phase in range(2):
                    row_at = 2 * row_phase + row_tap - 1
                    col_at = 2 * col_phase + col_tap - 1
                    part = plane[(row_at % 4) * 4 + col_at % 4]
                    left = (row_phase * 2 + col_phase) * cells
                    taps[top : top + channels, left : left + cells] = moved_cells(
                        part, row_at < 0, col_at < 0, row_len
                    )


def greet(axes):
    barrier = pltpu.get_barrier_semaphore()
    total = 0
    for axis, size in axes:
        me = lax.axis_index(axis)
        for k in range(1, size):
            pl.semaphore_signal(
                barrier, inc=1, device_id={axis: (me + k) % size}, device_id_type=pl.DeviceIdType.MESH
            )
        total += size - 1
    pl.semaphore_wait(barrier, total)


def to_device(src, dst, send_sem, recv_sem, axis, peer):
    return pltpu.make_async_remote_copy(
        src_ref=src,
        dst_ref=dst,
        send_sem=send_sem,
        recv_sem=recv_sem,
        device_id={axis: peer},
        device_id_type=pl.DeviceIdType.MESH,
    )


def first_kernel(
    n, row_len, chunks,
    vol, w, pre, hid_out,
    taps, part, rim, hid_send, hid_recv, rim_send_sem, rim_recv_sem, send_sem, recv_sem,
):
    me = lax.axis_index("space")
    channels = vol.shape[2]
    rows = 9 * channels
    out_channels = w.shape[1]
    wide = out_channels // chunks
    group = out_channels // n
    per_chunk = n // chunks
    greet([("space", n)])

    fill_taps(vol.at[1], taps, row_len)

    def rim_copy(c):
        cut = pl.ds(c * wide, wide)
        return to_device(
            part.at[cut], rim.at[cut], rim_send_sem.at[c], rim_recv_sem.at[c], "space", (me + 1) % n
        )

    for c in range(chunks):
        cut = slice(c * wide, (c + 1) * wide)
        part[cut, :] = contract_first(w[0:rows, cut], taps[...]).astype(part.dtype)

        @pl.when(me < n - 1)
        def _():
            rim_copy(c).start()

    pre[...] = contract_first(w[2 * rows : 3 * rows, :], taps[...])
    fill_taps(vol.at[0], taps, row_len)
    pre[...] += contract_first(w[rows : 2 * rows, :], taps[...])

    def hid_copy(peer):
        return to_device(
            hid_send.at[peer], hid_recv.at[me], send_sem.at[peer], recv_sem.at[me], "space", peer
        )

    def hid_arrival(source):
        return to_device(
            hid_send.at[source], hid_recv.at[source], send_sem.at[source], recv_sem.at[source], "space", source
        )

    for c in range(chunks):
        cut = slice(c * wide, (c + 1) * wide)

        @pl.when(me > 0)
        def _():
            rim_copy(c).wait_recv()
            pre[cut, :] += rim[cut, :].astype(jnp.float32)

        for g in range(per_chunk):
            at = c * per_chunk + g
            hid_send[at] = activate(pre[at * group : (at + 1) * group, :]).astype(hid_send.dtype)
        for k in range(per_chunk):
            peer = c * per_chunk + (me + k + 1) % per_chunk

            @pl.when(peer != me)
            def _():
                hid_copy(peer).start()

    for k in range(1, n):
        hid_arrival((me + k) % n).wait_recv()
    hid_recv[me] = hid_send[me]
    hid_out[...] = hid_recv[...]
    for k in range(1, n):
        hid_copy((me + k) % n).wait_send()

    @pl.when(me < n - 1)
    def _():
        for c in range(chunks):
            rim_copy(c).wait_send()


def second_kernel(
    n, m, row_len,
    hid, w, cot, grad, back_out,
    taps, terms, back_send, back_recv, sum_send, sum_recv, all_send, all_recv,
    back_send_sem, back_recv_sem, sum_send_sem, sum_recv_sem, all_send_sem, all_recv_sem,
):
    me = lax.axis_index("space")
    mine = lax.axis_index("dp")
    depth, group, _ = hid.shape
    cells = row_len * (hid.shape[2] // 4 // row_len)
    planes = depth // 2
    quarter = cot.shape[0] // m
    greet([("space", n), ("dp", m)])

    def cell_block(a, b, c, s):
        top = ((a * 3 + b) * 3 + c) * group
        return (slice(top, top + group), slice(s * cells, (s + 1) * cells))

    for x in range(depth):
        for b in range(3):
            for c in range(3):
                phase = 2 * ((b + 1) % 2) + (c + 1) % 2
                value = moved_cells(
                    hid[x, :, phase * cells : (phase + 1) * cells], b == 0, c == 0, row_len
                )
                if x % 2 == 0:
                    taps[cell_block(1, b, c, x // 2)] = value
                else:
                    taps[cell_block(2, b, c, x // 2)] = value
                    if x // 2 + 1 < planes:
                        taps[cell_block(0, b, c, x // 2 + 1)] = value
                if x == 0:
                    taps[cell_block(0, b, c, 0)] = jnp.zeros_like(value)

    def sum_copy(peer):
        return to_device(
            sum_send.at[peer], sum_recv.at[mine], sum_send_sem.at[peer], sum_recv_sem.at[mine], "dp", peer
        )

    def all_copy(peer):
        return to_device(
            all_send, all_recv.at[mine], all_send_sem.at[peer], all_recv_sem.at[mine], "dp", peer
        )

    def quarter_of(owner):
        cut = pl.ds(pl.multiple_of(owner * quarter, quarter), quarter)
        return contract_last(taps[...], cot[cut, :])

    for k in range(1, m):
        peer = (mine + k) % m
        sum_send[peer] = quarter_of(peer).astype(sum_send.dtype)
        sum_copy(peer).start()

    terms[...] = jnp.dot(w[...], cot[...], preferred_element_type=jnp.float32)

    def term(x, b, c):
        if x % 2 == 0:
            return terms[cell_block(1, b, c, x // 2)]
        value = terms[cell_block(2, b, c, x // 2)]
        if x // 2 + 1 < planes:
            value = value + terms[cell_block(0, b, c, x // 2 + 1)]
        return value

    def back_copy(peer):
        return to_device(
            back_send.at[peer], back_recv.at[me], back_send_sem.at[peer], back_recv_sem.at[me], "space", peer
        )

    for x in range(depth):
        corner = term(x, 0, 2) + moved_back(term(x, 0, 0), False, True, row_len)
        phases = [
            term(x, 1, 1),
            term(x, 1, 2) + moved_back(term(x, 1, 0), False, True, row_len),
            term(x, 2, 1) + moved_back(term(x, 0, 1), True, False, row_len),
            term(x, 2, 2)
            + moved_back(term(x, 2, 0), False, True, row_len)
            + moved_back(corner, True, False, row_len),
        ]
        for phase in range(4):
            back_send[x, :, phase * cells : (phase + 1) * cells] = phases[phase].astype(back_send.dtype)
    for k in range(1, n):
        back_copy((me + k) % n).start()

    own = quarter_of(mine)
    own_cut = pl.ds(pl.multiple_of(mine * quarter, quarter), quarter)
    for k in range(1, m):
        source = (mine + k) % m
        to_device(
            sum_send.at[source], sum_recv.at[source], sum_send_sem.at[source], sum_recv_sem.at[source], "dp", source
        ).wait_recv()
        own = own + sum_recv[source].astype(jnp.float32)
    grad[:, own_cut] = own
    all_send[...] = own.astype(all_send.dtype)
    for k in range(1, m):
        all_copy((mine + k) % m).start()

    back_recv[me] = back_send[me]
    for k in range(1, n):
        source = (me + k) % n
        to_device(
            back_send.at[source], back_recv.at[source], back_send_sem.at[source], back_recv_sem.at[source], "space", source
        ).wait_recv()
    back_out[...] = back_recv[...]
    for k in range(1, m):
        source = (mine + k) % m
        to_device(
            all_send, all_recv.at[source], all_send_sem.at[source], all_recv_sem.at[source], "dp", source
        ).wait_recv()
        cut = pl.ds(pl.multiple_of(source * quarter, quarter), quarter)
        grad[:, cut] = all_recv[source].astype(jnp.float32)
    for k in range(1, n):
        back_copy((me + k) % n).wait_send()
    for k in range(1, m):
        sum_copy((mine + k) % m).wait_send()
        all_copy((mine + k) % m).wait_send()


def in_vmem(count):
    return [pl.BlockSpec(memory_space=pltpu.VMEM)] * count


def per_device(volume, w_first, w_second, cotangent):
    n = lax.axis_size("space")
    m = lax.axis_size("dp")
    channels = volume.shape[1]
    cells = volume.shape[4]
    out_channels = w_first.shape[4]
    group = w_second.shape[3]
    last = w_second.shape[4]
    row_len = WID // 4
    if volume.shape[2] != 2 or group % 16 or (last // m) % 128 or n % 2:
        return plain_device(volume, w_first, w_second, cotangent)
    planes = jnp.transpose(volume[0], (1, 2, 0, 3))
    w_flat = w_first.reshape(27 * channels, out_channels)
    span = 4 * cells
    chunks = 2
    pre, hidden = pl.pallas_call(
        functools.partial(first_kernel, n, row_len, chunks),
        out_shape=(
            jax.ShapeDtypeStruct((out_channels, span), jnp.float32),
            jax.ShapeDtypeStruct((n, group, span), jnp.bfloat16),
        ),
        in_specs=in_vmem(2),
        out_specs=tuple(in_vmem(2)),
        scratch_shapes=[
            pltpu.VMEM((9 * channels, span), jnp.bfloat16),
            pltpu.VMEM((out_channels, span), jnp.bfloat16),
            pltpu.VMEM((out_channels, span), jnp.bfloat16),
            pltpu.VMEM((n, group, span), jnp.bfloat16),
            pltpu.VMEM((n, group, span), jnp.bfloat16),
            pltpu.SemaphoreType.DMA((chunks,)),
            pltpu.SemaphoreType.DMA((chunks,)),
            pltpu.SemaphoreType.DMA((n,)),
            pltpu.SemaphoreType.DMA((n,)),
        ],
        compiler_params=pltpu.CompilerParams(
            collective_id=0, has_side_effects=True, vmem_limit_bytes=40 * 2**20
        ),
        cost_estimate=pl.CostEstimate(
            flops=2 * 27 * channels * out_channels * span, bytes_accessed=6 * 2**20, transcendentals=0
        ),
    )(planes, w_flat)
    cot = lax.all_gather(cotangent[0].reshape(cotangent.shape[1], -1), "space", axis=0, tiled=True)
    rows = 27 * group
    out_cells = cot.shape[1]
    grad, back = pl.pallas_call(
        functools.partial(second_kernel, n, m, row_len),
        out_shape=(
            jax.ShapeDtypeStruct((rows, last), jnp.float32),
            jax.ShapeDtypeStruct((n, group, span), jnp.bfloat16),
        ),
        in_specs=in_vmem(3),
        out_specs=tuple(in_vmem(2)),
        scratch_shapes=[
            pltpu.VMEM((rows, out_cells), jnp.bfloat16),
            pltpu.VMEM((rows, out_cells), jnp.float32),
            pltpu.VMEM((n, group, span), jnp.bfloat16),
            pltpu.VMEM((n, group, span), jnp.bfloat16),
            pltpu.VMEM((m, rows, last // m), jnp.bfloat16),
            pltpu.VMEM((m, rows, last // m), jnp.bfloat16),
            pltpu.VMEM((rows, last // m), jnp.bfloat16),
            pltpu.VMEM((m, rows, last // m), jnp.bfloat16),
            pltpu.SemaphoreType.DMA((n,)),
            pltpu.SemaphoreType.DMA((n,)),
            pltpu.SemaphoreType.DMA((m,)),
            pltpu.SemaphoreType.DMA((m,)),
            pltpu.SemaphoreType.DMA((m,)),
            pltpu.SemaphoreType.DMA((m,)),
        ],
        compiler_params=pltpu.CompilerParams(
            collective_id=1, has_side_effects=True, vmem_limit_bytes=40 * 2**20
        ),
        cost_estimate=pl.CostEstimate(
            flops=4 * rows * last * out_cells, bytes_accessed=6 * 2**20, transcendentals=0
        ),
    )(hidden, w_second.reshape(rows, last), cot)
    hidden_grad = back.reshape(out_channels, span)
    pre_grad = (hidden_grad.astype(jnp.float32) * slope_of(pre)).astype(jnp.bfloat16)
    return (
        grad.reshape(3, 3, 3, group, last),
        pre_grad.reshape(1, out_channels, 1, 4, cells),
    )


def solution(mesh):
    in_specs = (
        P("dp", None, "space", None, None),
        P(),
        P(None, None, None, "space", None),
        P("dp", "space", None, None),
    )
    out_specs = (P(None, None, None, "space", None), P("dp", None, "space", None, None))
    return jax.shard_map(
        per_device, mesh=mesh, in_specs=in_specs, out_specs=out_specs, check_vma=False
    )
```

```python
import functools

import jax
import jax.numpy as jnp
from jax import lax
from jax.experimental import pallas as pl
from jax.experimental.pallas import tpu as pltpu
from jax.sharding import PartitionSpec as P

C3 = 512
WID = 128


leak_slope = 0.3


def from_behind(block, axis, distance):
    devices = range(lax.axis_size(axis))
    route = [(i - distance, i) for i in devices if i - distance in devices]
    return lax.ppermute(block, axis, route)


def activate(values):
    return leak_slope * values + (1.0 - leak_slope) * values * jax.nn.sigmoid(values)


def slope_of(values):
    sigmoid_value = jax.nn.sigmoid(values)
    return leak_slope + (1.0 - leak_slope) * (
        sigmoid_value + values * sigmoid_value * (1.0 - sigmoid_value)
    )


def stride_taps(values, along_dim):
    length = values.shape[along_dim] // 2
    paired = values.reshape(values.shape[:along_dim] + (length, 2) + values.shape[along_dim + 1 :])
    even_cells = lax.index_in_dim(paired, 0, along_dim + 1, keepdims=False)
    odd_cells = lax.index_in_dim(paired, 1, along_dim + 1, keepdims=False)
    before = jnp.concatenate(
        [
            jnp.zeros_like(lax.slice_in_dim(odd_cells, 0, 1, axis=along_dim)),
            lax.slice_in_dim(odd_cells, 0, length - 1, axis=along_dim),
        ],
        along_dim,
    )
    return [before, even_cells, odd_cells]


def step_cells(values, by_row, by_col, row_len):
    cells = values.shape[-1]
    if by_row:
        filler = jnp.zeros(values.shape[:-1] + (row_len,), values.dtype)
        values = jnp.concatenate([filler, values[..., : cells - row_len]], -1)
    if by_col:
        filler = jnp.zeros(values.shape[:-1] + (1,), values.dtype)
        moved = jnp.concatenate([filler, values[..., : cells - 1]], -1)
        keeper = lax.iota(jnp.int32, cells) % row_len != 0
        values = jnp.where(keeper, moved, jnp.zeros_like(moved))
    return values


def plane_taps(values, row_len):
    phases = values.shape[-2]
    out_phases = phases // 2
    collected = []
    for row_tap in range(3):
        for col_tap in range(3):
            rows_out = []
            for row_phase in range(out_phases):
                cols_out = []
                for col_phase in range(out_phases):
                    row_at = 2 * row_phase + row_tap - 1
                    col_at = 2 * col_phase + col_tap - 1
                    part = values[..., row_at % phases, col_at % phases, :]
                    cols_out.append(step_cells(part, row_at < 0, col_at < 0, row_len))
                rows_out.append(jnp.stack(cols_out, -2))
            collected.append(jnp.stack(rows_out, -3))
    return collected


def all_taps(values, row_len):
    collected = []
    for depth_part in stride_taps(values, 1):
        collected.extend(plane_taps(depth_part, row_len))
    return collected


def contract_first(left_side, right_side):
    return lax.dot_general(
        left_side, right_side, (((0,), (0,)), ((), ())), preferred_element_type=jnp.float32
    )


def contract_last(left_side, right_side):
    return lax.dot_general(
        left_side, right_side, (((1,), (1,)), ((), ())), preferred_element_type=jnp.float32
    )


def plain_device(volume, w_first, w_second, cotangent):
    channels = volume.shape[1]
    depth_cells = volume.shape[2]
    cell_count = volume.shape[4]
    half_depth = depth_cells // 2
    out_channels = w_first.shape[4]
    row_len = WID // 4
    paired = volume[0].reshape(channels, half_depth, 2, 4, 4, cell_count)
    even_cells = paired[:, :, 0]
    odd_cells = paired[:, :, 1]
    w_flat = w_first.reshape(27 * channels, out_channels)
    rim_cells = from_behind(odd_cells, "space", 1)
    before = jnp.concatenate([rim_cells, odd_cells[:, : half_depth - 1]], 1)
    collected = []
    for depth_part in (before, even_cells, odd_cells):
        collected.extend(plane_taps(depth_part, row_len))
    stacked = jnp.stack(collected, 0).reshape(27 * channels, -1)
    pre_act = contract_first(w_flat, stacked).reshape(out_channels, half_depth, 4, cell_count)
    hidden = activate(pre_act).astype(jnp.bfloat16)
    by_channel = lax.all_to_all(hidden, "space", split_axis=0, concat_axis=1, tiled=True)
    own_channels = by_channel.shape[0]
    full_depth = by_channel.shape[1]
    hidden_cells = by_channel.reshape(own_channels, full_depth, 2, 2, cell_count)
    hidden_taps = jnp.stack(all_taps(hidden_cells, row_len), 0).reshape(27 * own_channels, -1)
    w_rows = w_second.reshape(27 * own_channels, C3)
    out_cells = hidden_taps.shape[1]
    gathered = lax.all_gather(cotangent[0], "space", axis=0, tiled=True)
    cot_flat = gathered.reshape(C3, out_cells)
    weight_grad = contract_last(hidden_taps, cot_flat)
    tap_terms = jnp.dot(w_rows, cot_flat, preferred_element_type=jnp.float32)
    grad_second = lax.psum(weight_grad, "dp").reshape(3, 3, 3, own_channels, C3)

    def spread(field):
        return jnp.stack(all_taps(field, row_len), 0).reshape(27 * own_channels, -1)

    unused, pull = jax.vjp(
        spread, jnp.zeros((own_channels, full_depth, 2, 2, cell_count), jnp.float32)
    )
    back_terms = pull(tap_terms)[0]
    back_terms = back_terms.astype(jnp.bfloat16).reshape(own_channels, full_depth, 4, cell_count)
    hidden_grad = lax.all_to_all(back_terms, "space", split_axis=1, concat_axis=0, tiled=True)
    pre_grad = (hidden_grad.astype(jnp.float32) * slope_of(pre_act)).astype(jnp.bfloat16)
    return (grad_second, pre_grad[None])


def moved_cells(block, by_row, by_col, row_len):
    if not (by_row or by_col):
        return block
    cells = block.shape[-1]
    at = lax.broadcasted_iota(jnp.int32, block.shape, 1)
    wide = block.astype(jnp.float32)
    if by_row:
        wide = jnp.where(at >= row_len, pltpu.roll(wide, row_len, 1), 0.0)
    if by_col:
        wide = jnp.where(at % row_len != 0, pltpu.roll(wide, 1, 1), 0.0)
    return wide.astype(block.dtype)


def moved_back(block, by_row, by_col, row_len):
    cells = block.shape[-1]
    at = lax.broadcasted_iota(jnp.int32, block.shape, 1)
    if by_row:
        block = pltpu.roll(jnp.where(at >= row_len, block, 0.0), cells - row_len, 1)
    if by_col:
        block = pltpu.roll(jnp.where(at % row_len != 0, block, 0.0), cells - 1, 1)
    return block


def fill_taps(plane, taps, row_len):
    _, channels, cells = plane.shape
    for row_tap in range(3):
        for col_tap in range(3):
            top = (row_tap * 3 + col_tap) * channels
            for row_phase in range(2):
                for col_phase in range(2):
                    row_at = 2 * row_phase + row_tap - 1
                    col_at = 2 * col_phase + col_tap - 1
                    part = plane[(row_at % 4) * 4 + col_at % 4]
                    left = (row_phase * 2 + col_phase) * cells
                    taps[top : top + channels, left : left + cells] = moved_cells(
                        part, row_at < 0, col_at < 0, row_len
                    )


def greet(axes):
    barrier = pltpu.get_barrier_semaphore()
    total = 0
    for axis, size in axes:
        me = lax.axis_index(axis)
        for k in range(1, size):
            pl.semaphore_signal(
                barrier, inc=1, device_id={axis: (me + k) % size}, device_id_type=pl.DeviceIdType.MESH
            )
        total += size - 1
    pl.semaphore_wait(barrier, total)


def to_device(src, dst, send_sem, recv_sem, axis, peer):
    return pltpu.make_async_remote_copy(
        src_ref=src,
        dst_ref=dst,
        send_sem=send_sem,
        recv_sem=recv_sem,
        device_id={axis: peer},
        device_id_type=pl.DeviceIdType.MESH,
    )


def section_kernel(
    n, m, row_len, chunks,
    vol, w1_hbm, w2_hbm, cot_own, grad, pre_grad,
    w1, w2, cot, taps, pre, part, rim, hid_send, hid_recv,
    out_taps, terms, back_send, back_recv, sum_send, sum_recv, all_send, all_recv,
    w1_sem, w2_sem, cot_send_sem, cot_recv_sem, rim_send_sem, rim_recv_sem, hid_send_sem, hid_recv_sem,
    back_send_sem, back_recv_sem, sum_send_sem, sum_recv_sem, all_send_sem, all_recv_sem,
):
    me = lax.axis_index("space")
    mine = lax.axis_index("dp")
    chips = n // 2
    chip = me // 2
    core = me % 2
    channels = vol.shape[2]
    cells = vol.shape[3]
    rows = 9 * channels
    out_channels = w1.shape[1]
    wide = out_channels // chunks
    group = out_channels // n
    per_chunk = n // chunks
    depth = n
    planes = depth // 2
    quarter = cot.shape[0] // m
    share = cot_own.shape[0]

    def w1_copy(a):
        cut = pl.ds(a * rows, rows)
        return pltpu.make_async_copy(w1_hbm.at[cut], w1.at[cut], w1_sem.at[a])

    for a in (0, 2, 1):
        w1_copy(a).start()
    w2_copy = pltpu.make_async_copy(w2_hbm, w2, w2_sem.at[0])
    w2_copy.start()
    own_rows = pl.ds(pl.multiple_of(me * share, share), share)
    for s in range(planes):
        cot[own_rows, s * cells : (s + 1) * cells] = cot_own[:, s, :]
    greet([("space", n), ("dp", m)])

    def cot_copy(block, way):
        cut = pl.ds(pl.multiple_of(block * share, share), share)
        peer = [(me + 2) % n, (me + n - 2) % n, 2 * chip + 1 - core][way]
        return to_device(
            cot.at[cut], cot.at[cut], cot_send_sem.at[way, block], cot_recv_sem.at[block], "space", peer
        )

    def cot_send(h, act):
        up = 2 * ((chip - h + chips) % chips) + core
        down = 2 * ((chip + h) % chips) + core

        @pl.when((chip - h >= 0) & (chip + 1 < chips))
        def _():
            act(cot_copy(up, 0))

        @pl.when((chip + h < chips) & (chip - 1 >= 0))
        def _():
            act(cot_copy(down, 1))

    def cot_pass(h, wait, act):
        up = 2 * ((chip - h + chips) % chips) + core
        down = 2 * ((chip + h) % chips) + core

        @pl.when(chip - h >= 0)
        def _():
            if wait:
                cot_copy(up, 2).wait_recv()
            act(cot_copy(up, 2))

        @pl.when(chip + h < chips)
        def _():
            if wait:
                cot_copy(down, 2).wait_recv()
            act(cot_copy(down, 2))

    start = lambda copy: copy.start()
    cot_copy(me, 2).start()
    cot_send(0, start)

    fill_taps(vol.at[1], taps, row_len)
    w1_copy(0).wait()

    def rim_copy(c):
        cut = pl.ds(c * wide, wide)
        return to_device(
            part.at[cut], rim.at[cut], rim_send_sem.at[c], rim_recv_sem.at[c], "space", (me + 1) % n
        )

    for c in range(chunks):
        cut = slice(c * wide, (c + 1) * wide)
        part[cut, :] = contract_first(w1[0:rows, cut], taps[...]).astype(part.dtype)

        @pl.when(me < n - 1)
        def _():
            rim_copy(c).start()

    w1_copy(2).wait()
    pre[...] = contract_first(w1[2 * rows : 3 * rows, :], taps[...])
    fill_taps(vol.at[0], taps, row_len)
    w1_copy(1).wait()
    pre[...] += contract_first(w1[rows : 2 * rows, :], taps[...])

    cot_pass(1, True, start)
    cot_send(1, start)

    def hid_copy(peer):
        return to_device(
            hid_send.at[peer], hid_recv.at[me], hid_send_sem.at[peer], hid_recv_sem.at[me], "space", peer
        )

    for c in range(chunks):
        cut = slice(c * wide, (c + 1) * wide)

        @pl.when(me > 0)
        def _():
            rim_copy(c).wait_recv()
            pre[cut, :] += rim[cut, :].astype(jnp.float32)

        for g in range(per_chunk):
            at = c * per_chunk + g
            hid_send[at] = activate(pre[at * group : (at + 1) * group, :]).astype(hid_send.dtype)
        for k in range(per_chunk):
            peer = c * per_chunk + (me + k + 1) % per_chunk

            @pl.when(peer != me)
            def _():
                hid_copy(peer).start()

    for h in range(2, chips):
        cot_pass(h, True, start)
        if h + 1 < chips:
            cot_send(h, start)
    hid_recv[me] = hid_send[me]
    for z in range(chips):
        cot_copy(2 * z + 1 - core, 2).wait_recv()

    def cell_block(a, b, c, s):
        top = ((a * 3 + b) * 3 + c) * group
        return (slice(top, top + group), slice(s * cells, (s + 1) * cells))

    w2_copy.wait()
    terms[...] = jnp.dot(w2[...], cot[...], preferred_element_type=jnp.float32)

    def term(x, b, c):
        if x % 2 == 0:
            return terms[cell_block(1, b, c, x // 2)]
        value = terms[cell_block(2, b, c, x // 2)]
        if x // 2 + 1 < planes:
            value = value + terms[cell_block(0, b, c, x // 2 + 1)]
        return value

    def back_copy(peer):
        return to_device(
            back_send.at[peer], back_recv.at[me], back_send_sem.at[peer], back_recv_sem.at[me], "space", peer
        )

    for x in range(depth):
        corner = term(x, 0, 2) + moved_back(term(x, 0, 0), False, True, row_len)
        phases = [
            term(x, 1, 1),
            term(x, 1, 2) + moved_back(term(x, 1, 0), False, True, row_len),
            term(x, 2, 1) + moved_back(term(x, 0, 1), True, False, row_len),
            term(x, 2, 2)
            + moved_back(term(x, 2, 0), False, True, row_len)
            + moved_back(corner, True, False, row_len),
        ]
        for phase in range(4):
            back_send[x, :, phase * cells : (phase + 1) * cells] = phases[phase].astype(back_send.dtype)
    for k in range(1, n):
        back_copy((me + k) % n).start()
    back_recv[me] = back_send[me]

    for k in range(1, n):
        source = (me + k) % n
        to_device(
            hid_send.at[source], hid_recv.at[source], hid_send_sem.at[source], hid_recv_sem.at[source], "space", source
        ).wait_recv()
    for x in range(depth):
        for b in range(3):
            for c in range(3):
                phase = 2 * ((b + 1) % 2) + (c + 1) % 2
                value = moved_cells(
                    hid_recv[x, :, phase * cells : (phase + 1) * cells], b == 0, c == 0, row_len
                )
                if x % 2 == 0:
                    out_taps[cell_block(1, b, c, x // 2)] = value
                else:
                    out_taps[cell_block(2, b, c, x // 2)] = value
                    if x // 2 + 1 < planes:
                        out_taps[cell_block(0, b, c, x // 2 + 1)] = value
                if x == 0:
                    out_taps[cell_block(0, b, c, 0)] = jnp.zeros_like(value)

    def sum_copy(peer):
        return to_device(
            sum_send.at[peer], sum_recv.at[mine], sum_send_sem.at[peer], sum_recv_sem.at[mine], "dp", peer
        )

    def all_copy(peer):
        return to_device(
            all_send, all_recv.at[mine], all_send_sem.at[peer], all_recv_sem.at[mine], "dp", peer
        )

    def columns(owner):
        return pl.ds(pl.multiple_of(owner * quarter, quarter), quarter)

    for k in range(1, m):
        peer = (mine + k) % m
        sum_send[peer] = contract_last(out_taps[...], cot[columns(peer), :]).astype(sum_send.dtype)
        sum_copy(peer).start()
    own = contract_last(out_taps[...], cot[columns(mine), :])
    for k in range(1, m):
        source = (mine + k) % m
        to_device(
            sum_send.at[source], sum_recv.at[source], sum_send_sem.at[source], sum_recv_sem.at[source], "dp", source
        ).wait_recv()
        own = own + sum_recv[source].astype(jnp.float32)
    all_send[...] = own.astype(all_send.dtype)
    for k in range(1, m):
        all_copy((mine + k) % m).start()
    grad[:, columns(mine)] = own

    for k in range(1, n):
        source = (me + k) % n
        to_device(
            back_send.at[source], back_recv.at[source], back_send_sem.at[source], back_recv_sem.at[source], "space", source
        ).wait_recv()
    for g in range(n):
        cut = slice(g * group, (g + 1) * group)
        pre_grad[cut, :] = (back_recv[g].astype(jnp.float32) * slope_of(pre[cut, :])).astype(pre_grad.dtype)
    for k in range(1, m):
        source = (mine + k) % m
        to_device(
            all_send, all_recv.at[source], all_send_sem.at[source], all_recv_sem.at[source], "dp", source
        ).wait_recv()
        grad[:, columns(source)] = all_recv[source].astype(jnp.float32)

    finish = lambda copy: copy.wait_send()
    cot_copy(me, 2).wait_send()
    for h in range(chips - 1):
        cot_send(h, finish)
        cot_pass(h + 1, False, finish)

    @pl.when(me < n - 1)
    def _():
        for c in range(chunks):
            rim_copy(c).wait_send()

    for k in range(1, n):
        hid_copy((me + k) % n).wait_send()
        back_copy((me + k) % n).wait_send()
    for k in range(1, m):
        sum_copy((mine + k) % m).wait_send()
        all_copy((mine + k) % m).wait_send()


def per_device(volume, w_first, w_second, cotangent):
    n = lax.axis_size("space")
    m = lax.axis_size("dp")
    channels = volume.shape[1]
    cells = volume.shape[4]
    out_channels = w_first.shape[4]
    group = w_second.shape[3]
    last = w_second.shape[4]
    row_len = WID // 4
    if volume.shape[2] != 2 or group % 16 or (last // m) % 128 or n % 2:
        return plain_device(volume, w_first, w_second, cotangent)
    planes = jnp.transpose(volume[0], (1, 2, 0, 3))
    span = 4 * cells
    chunks = 2
    rows = 27 * group
    cot_planes = cotangent.shape[2]
    out_cells = cot_planes * cells
    quarter = last // m
    bf16, f32 = jnp.bfloat16, jnp.float32
    vmem = pl.BlockSpec(memory_space=pltpu.VMEM)
    anywhere = pl.BlockSpec(memory_space=pl.ANY)
    dma = pltpu.SemaphoreType.DMA
    grad, pre_grad = pl.pallas_call(
        functools.partial(section_kernel, n, m, row_len, chunks),
        out_shape=(
            jax.ShapeDtypeStruct((rows, last), f32),
            jax.ShapeDtypeStruct((out_channels, span), bf16),
        ),
        in_specs=[vmem, anywhere, anywhere, vmem],
        out_specs=(vmem, vmem),
        scratch_shapes=[
            pltpu.VMEM((27 * channels, out_channels), bf16),
            pltpu.VMEM((rows, last), bf16),
            pltpu.VMEM((last, out_cells), bf16),
            pltpu.VMEM((9 * channels, span), bf16),
            pltpu.VMEM((out_channels, span), f32),
            pltpu.VMEM((out_channels, span), bf16),
            pltpu.VMEM((out_channels, span), bf16),
            pltpu.VMEM((n, group, span), bf16),
            pltpu.VMEM((n, group, span), bf16),
            pltpu.VMEM((rows, out_cells), bf16),
            pltpu.VMEM((rows, out_cells), f32),
            pltpu.VMEM((n, group, span), bf16),
            pltpu.VMEM((n, group, span), bf16),
            pltpu.VMEM((m, rows, quarter), bf16),
            pltpu.VMEM((m, rows, quarter), bf16),
            pltpu.VMEM((rows, quarter), bf16),
            pltpu.VMEM((m, rows, quarter), bf16),
            dma((3,)),
            dma((1,)),
            dma((3, n)),
            dma((n,)),
            dma((chunks,)),
            dma((chunks,)),
            dma((n,)),
            dma((n,)),
            dma((n,)),
            dma((n,)),
            dma((m,)),
            dma((m,)),
            dma((m,)),
            dma((m,)),
        ],
        compiler_params=pltpu.CompilerParams(
            collective_id=0, has_side_effects=True, vmem_limit_bytes=50 * 2**20
        ),
        cost_estimate=pl.CostEstimate(
            flops=2 * 27 * channels * out_channels * span + 4 * rows * last * out_cells,
            bytes_accessed=10 * 2**20,
            transcendentals=0,
        ),
    )(
        planes,
        w_first.reshape(27 * channels, out_channels),
        w_second.reshape(rows, last),
        cotangent[0],
    )
    return (
        grad.reshape(3, 3, 3, group, last),
        pre_grad.reshape(1, out_channels, 1, 4, cells),
    )


def solution(mesh):
    in_specs = (
        P("dp", None, "space", None, None),
        P(),
        P(None, None, None, "space", None),
        P("dp", "space", None, None),
    )
    out_specs = (P(None, None, None, "space", None), P("dp", None, "space", None, None))
    return jax.shard_map(
        per_device, mesh=mesh, in_specs=in_specs, out_specs=out_specs, check_vma=False
    )
```

```python
import functools

import jax
import jax.numpy as jnp
from jax import lax
from jax.experimental import pallas as pl
from jax.experimental.pallas import tpu as pltpu
from jax.sharding import PartitionSpec as P

C3 = 512
WID = 128


leak_slope = 0.3


def from_behind(block, axis, distance):
    devices = range(lax.axis_size(axis))
    route = [(i - distance, i) for i in devices if i - distance in devices]
    return lax.ppermute(block, axis, route)


def activate(values):
    return leak_slope * values + (1.0 - leak_slope) * values * jax.nn.sigmoid(values)


def slope_of(values):
    sigmoid_value = jax.nn.sigmoid(values)
    return leak_slope + (1.0 - leak_slope) * (
        sigmoid_value + values * sigmoid_value * (1.0 - sigmoid_value)
    )


def stride_taps(values, along_dim):
    length = values.shape[along_dim] // 2
    paired = values.reshape(values.shape[:along_dim] + (length, 2) + values.shape[along_dim + 1 :])
    even_cells = lax.index_in_dim(paired, 0, along_dim + 1, keepdims=False)
    odd_cells = lax.index_in_dim(paired, 1, along_dim + 1, keepdims=False)
    before = jnp.concatenate(
        [
            jnp.zeros_like(lax.slice_in_dim(odd_cells, 0, 1, axis=along_dim)),
            lax.slice_in_dim(odd_cells, 0, length - 1, axis=along_dim),
        ],
        along_dim,
    )
    return [before, even_cells, odd_cells]


def step_cells(values, by_row, by_col, row_len):
    cells = values.shape[-1]
    if by_row:
        filler = jnp.zeros(values.shape[:-1] + (row_len,), values.dtype)
        values = jnp.concatenate([filler, values[..., : cells - row_len]], -1)
    if by_col:
        filler = jnp.zeros(values.shape[:-1] + (1,), values.dtype)
        moved = jnp.concatenate([filler, values[..., : cells - 1]], -1)
        keeper = lax.iota(jnp.int32, cells) % row_len != 0
        values = jnp.where(keeper, moved, jnp.zeros_like(moved))
    return values


def plane_taps(values, row_len):
    phases = values.shape[-2]
    out_phases = phases // 2
    collected = []
    for row_tap in range(3):
        for col_tap in range(3):
            rows_out = []
            for row_phase in range(out_phases):
                cols_out = []
                for col_phase in range(out_phases):
                    row_at = 2 * row_phase + row_tap - 1
                    col_at = 2 * col_phase + col_tap - 1
                    part = values[..., row_at % phases, col_at % phases, :]
                    cols_out.append(step_cells(part, row_at < 0, col_at < 0, row_len))
                rows_out.append(jnp.stack(cols_out, -2))
            collected.append(jnp.stack(rows_out, -3))
    return collected


def all_taps(values, row_len):
    collected = []
    for depth_part in stride_taps(values, 1):
        collected.extend(plane_taps(depth_part, row_len))
    return collected


def contract_first(left_side, right_side):
    return lax.dot_general(
        left_side, right_side, (((0,), (0,)), ((), ())), preferred_element_type=jnp.float32
    )


def contract_last(left_side, right_side):
    return lax.dot_general(
        left_side, right_side, (((1,), (1,)), ((), ())), preferred_element_type=jnp.float32
    )


def plain_device(volume, w_first, w_second, cotangent):
    channels = volume.shape[1]
    depth_cells = volume.shape[2]
    cell_count = volume.shape[4]
    half_depth = depth_cells // 2
    out_channels = w_first.shape[4]
    row_len = WID // 4
    paired = volume[0].reshape(channels, half_depth, 2, 4, 4, cell_count)
    even_cells = paired[:, :, 0]
    odd_cells = paired[:, :, 1]
    w_flat = w_first.reshape(27 * channels, out_channels)
    rim_cells = from_behind(odd_cells, "space", 1)
    before = jnp.concatenate([rim_cells, odd_cells[:, : half_depth - 1]], 1)
    collected = []
    for depth_part in (before, even_cells, odd_cells):
        collected.extend(plane_taps(depth_part, row_len))
    stacked = jnp.stack(collected, 0).reshape(27 * channels, -1)
    pre_act = contract_first(w_flat, stacked).reshape(out_channels, half_depth, 4, cell_count)
    hidden = activate(pre_act).astype(jnp.bfloat16)
    by_channel = lax.all_to_all(hidden, "space", split_axis=0, concat_axis=1, tiled=True)
    own_channels = by_channel.shape[0]
    full_depth = by_channel.shape[1]
    hidden_cells = by_channel.reshape(own_channels, full_depth, 2, 2, cell_count)
    hidden_taps = jnp.stack(all_taps(hidden_cells, row_len), 0).reshape(27 * own_channels, -1)
    w_rows = w_second.reshape(27 * own_channels, C3)
    out_cells = hidden_taps.shape[1]
    gathered = lax.all_gather(cotangent[0], "space", axis=0, tiled=True)
    cot_flat = gathered.reshape(C3, out_cells)
    weight_grad = contract_last(hidden_taps, cot_flat)
    tap_terms = jnp.dot(w_rows, cot_flat, preferred_element_type=jnp.float32)
    grad_second = lax.psum(weight_grad, "dp").reshape(3, 3, 3, own_channels, C3)

    def spread(field):
        return jnp.stack(all_taps(field, row_len), 0).reshape(27 * own_channels, -1)

    unused, pull = jax.vjp(
        spread, jnp.zeros((own_channels, full_depth, 2, 2, cell_count), jnp.float32)
    )
    back_terms = pull(tap_terms)[0]
    back_terms = back_terms.astype(jnp.bfloat16).reshape(own_channels, full_depth, 4, cell_count)
    hidden_grad = lax.all_to_all(back_terms, "space", split_axis=1, concat_axis=0, tiled=True)
    pre_grad = (hidden_grad.astype(jnp.float32) * slope_of(pre_act)).astype(jnp.bfloat16)
    return (grad_second, pre_grad[None])


def moved_cells(block, by_row, by_col, row_len):
    if not (by_row or by_col):
        return block
    cells = block.shape[-1]
    at = lax.broadcasted_iota(jnp.int32, block.shape, 1)
    wide = block.astype(jnp.float32)
    if by_row:
        wide = jnp.where(at >= row_len, pltpu.roll(wide, row_len, 1), 0.0)
    if by_col:
        wide = jnp.where(at % row_len != 0, pltpu.roll(wide, 1, 1), 0.0)
    return wide.astype(block.dtype)


def moved_back(block, by_row, by_col, row_len):
    cells = block.shape[-1]
    at = lax.broadcasted_iota(jnp.int32, block.shape, 1)
    if by_row:
        block = pltpu.roll(jnp.where(at >= row_len, block, 0.0), cells - row_len, 1)
    if by_col:
        block = pltpu.roll(jnp.where(at % row_len != 0, block, 0.0), cells - 1, 1)
    return block


def fill_taps(plane, taps, row_len):
    _, channels, cells = plane.shape
    for row_tap in range(3):
        for col_tap in range(3):
            top = (row_tap * 3 + col_tap) * channels
            for row_phase in range(2):
                for col_phase in range(2):
                    row_at = 2 * row_phase + row_tap - 1
                    col_at = 2 * col_phase + col_tap - 1
                    part = plane[(row_at % 4) * 4 + col_at % 4]
                    left = (row_phase * 2 + col_phase) * cells
                    taps[top : top + channels, left : left + cells] = moved_cells(
                        part, row_at < 0, col_at < 0, row_len
                    )


def greet(axes):
    barrier = pltpu.get_barrier_semaphore()
    for axis, size in axes:
        me = lax.axis_index(axis)
        for k in range(1, size):
            pl.semaphore_signal(
                barrier, inc=1, device_id={axis: (me + k) % size}, device_id_type=pl.DeviceIdType.MESH
            )


def await_greetings(axes):
    pl.semaphore_wait(pltpu.get_barrier_semaphore(), sum(size - 1 for _, size in axes))


def to_device(src, dst, send_sem, recv_sem, axis, peer):
    return pltpu.make_async_remote_copy(
        src_ref=src,
        dst_ref=dst,
        send_sem=send_sem,
        recv_sem=recv_sem,
        device_id={axis: peer},
        device_id_type=pl.DeviceIdType.MESH,
    )


def section_kernel(
    n, m, row_len, chunks,
    vol, w1_hbm, w2_hbm, cot_own, grad, pre_grad,
    w1, w2, cot, taps, pre, part, rim, hid_send, hid_recv,
    out_taps, terms, back_send, back_recv, sum_send, sum_recv, all_send, all_recv,
    w1_sem, w2_sem, cot_send_sem, cot_recv_sem, rim_send_sem, rim_recv_sem, hid_send_sem, hid_recv_sem,
    back_send_sem, back_recv_sem, sum_send_sem, sum_recv_sem, all_send_sem, all_recv_sem,
):
    me = lax.axis_index("space")
    mine = lax.axis_index("dp")
    chips = n // 2
    chip = me // 2
    core = me % 2
    channels = vol.shape[2]
    cells = vol.shape[3]
    rows = 9 * channels
    out_channels = w1.shape[1]
    wide = out_channels // chunks
    group = out_channels // n
    half = group // chunks
    tap_rows = 27 * half
    depth = n
    planes = depth // 2
    quarter = cot.shape[0] // m
    share = cot_own.shape[0]

    def w1_copy(a):
        cut = pl.ds(a * rows, rows)
        return pltpu.make_async_copy(w1_hbm.at[cut], w1.at[cut], w1_sem.at[a])

    axes = [("space", n), ("dp", m)]
    greet(axes)
    for a in (0, 2, 1):
        w1_copy(a).start()
    w2_copy = pltpu.make_async_copy(w2_hbm, w2, w2_sem.at[0])
    w2_copy.start()
    own_rows = pl.ds(pl.multiple_of(me * share, share), share)
    for s in range(planes):
        cot[own_rows, s * cells : (s + 1) * cells] = cot_own[:, s, :]
    fill_taps(vol.at[1], taps, row_len)
    await_greetings(axes)

    def cot_copy(block, way):
        cut = pl.ds(pl.multiple_of(block * share, share), share)
        peer = [(me + 2) % n, (me + n - 2) % n, 2 * chip + 1 - core][way]
        return to_device(
            cot.at[cut], cot.at[cut], cot_send_sem.at[way, block], cot_recv_sem.at[block], "space", peer
        )

    def cot_send(h, act):
        up = 2 * ((chip - h + chips) % chips) + core
        down = 2 * ((chip + h) % chips) + core

        @pl.when((chip - h >= 0) & (chip + 1 < chips))
        def _():
            act(cot_copy(up, 0))

        @pl.when((chip + h < chips) & (chip - 1 >= 0))
        def _():
            act(cot_copy(down, 1))

    def cot_pass(h, wait, act):
        up = 2 * ((chip - h + chips) % chips) + core
        down = 2 * ((chip + h) % chips) + core

        @pl.when(chip - h >= 0)
        def _():
            if wait:
                cot_copy(up, 2).wait_recv()
            act(cot_copy(up, 2))

        @pl.when(chip + h < chips)
        def _():
            if wait:
                cot_copy(down, 2).wait_recv()
            act(cot_copy(down, 2))

    start = lambda copy: copy.start()
    cot_copy(me, 2).start()
    cot_send(0, start)

    w1_copy(0).wait()

    def rim_copy(c):
        cut = pl.ds(c * wide, wide)
        return to_device(
            part.at[cut], rim.at[cut], rim_send_sem.at[c], rim_recv_sem.at[c], "space", (me + 1) % n
        )

    before = contract_first(w1[0:rows, :], taps[...])
    for c in range(chunks):
        for g in range(n):
            from_row = g * group + c * half
            to_row = c * wide + g * half
            part[to_row : to_row + half, :] = before[from_row : from_row + half].astype(part.dtype)

        @pl.when(me < n - 1)
        def _():
            rim_copy(c).start()

    w1_copy(2).wait()
    pre[...] = contract_first(w1[2 * rows : 3 * rows, :], taps[...])
    fill_taps(vol.at[0], taps, row_len)
    w1_copy(1).wait()
    pre[...] += contract_first(w1[rows : 2 * rows, :], taps[...])

    cot_pass(1, True, start)
    cot_send(1, start)

    def hid_copy(c, peer):
        return to_device(
            hid_send.at[c, peer], hid_recv.at[c, me], hid_send_sem.at[c, peer], hid_recv_sem.at[c, me], "space", peer
        )

    for c in range(chunks):

        @pl.when(me > 0)
        def _():
            rim_copy(c).wait_recv()
            for g in range(n):
                to_row = g * group + c * half
                from_row = c * wide + g * half
                pre[to_row : to_row + half, :] += rim[from_row : from_row + half, :].astype(jnp.float32)

        for g in range(n):
            at = g * group + c * half
            hid_send[c, g] = activate(pre[at : at + half, :]).astype(hid_send.dtype)
        for k in range(1, n):
            hid_copy(c, (me + k) % n).start()

    for h in range(2, chips):
        cot_pass(h, True, start)
        if h + 1 < chips:
            cot_send(h, start)
    for c in range(chunks):
        hid_recv[c, me] = hid_send[c, me]
    for z in range(chips):
        cot_copy(2 * z + 1 - core, 2).wait_recv()

    def cell_block(a, b, c, s):
        top = ((a * 3 + b) * 3 + c) * group
        return (slice(top, top + group), slice(s * cells, (s + 1) * cells))

    def sum_copy(c, peer):
        return to_device(
            sum_send.at[c, peer], sum_recv.at[c, mine], sum_send_sem.at[c, peer], sum_recv_sem.at[c, mine], "dp", peer
        )

    def all_copy(c, peer):
        return to_device(
            all_send.at[c], all_recv.at[c, mine], all_send_sem.at[c, peer], all_recv_sem.at[c, mine], "dp", peer
        )

    def columns(owner):
        return pl.ds(pl.multiple_of(owner * quarter, quarter), quarter)

    def await_hidden(c):
        for k in range(1, n):
            source = (me + k) % n
            to_device(
                hid_send.at[c, source], hid_recv.at[c, source],
                hid_send_sem.at[c, source], hid_recv_sem.at[c, source], "space", source,
            ).wait_recv()

    def weight_part(c):
        def tap_block(a, b, e, s):
            top = c * tap_rows + ((a * 3 + b) * 3 + e) * half
            return (slice(top, top + half), slice(s * cells, (s + 1) * cells))

        for x in range(depth):
            for b in range(3):
                for e in range(3):
                    phase = 2 * ((b + 1) % 2) + (e + 1) % 2
                    value = moved_cells(
                        hid_recv[c, x, :, phase * cells : (phase + 1) * cells], b == 0, e == 0, row_len
                    )
                    if x % 2 == 0:
                        out_taps[tap_block(1, b, e, x // 2)] = value
                    else:
                        out_taps[tap_block(2, b, e, x // 2)] = value
                        if x // 2 + 1 < planes:
                            out_taps[tap_block(0, b, e, x // 2 + 1)] = value
                    if x == 0:
                        out_taps[tap_block(0, b, e, 0)] = jnp.zeros_like(value)
        mine_taps = slice(c * tap_rows, (c + 1) * tap_rows)
        for k in range(1, m):
            peer = (mine + k) % m
            sum_send[c, peer] = contract_last(out_taps[mine_taps, :], cot[columns(peer), :]).astype(sum_send.dtype)
            sum_copy(c, peer).start()
        own = contract_last(out_taps[mine_taps, :], cot[columns(mine), :])
        grad[:, c * half : (c + 1) * half, columns(mine)] = own.reshape(27, half, quarter)

    def sum_part(c):
        at = slice(c * half, (c + 1) * half)
        own = grad[:, at, columns(mine)].reshape(tap_rows, quarter)
        for k in range(1, m):
            source = (mine + k) % m
            to_device(
                sum_send.at[c, source], sum_recv.at[c, source],
                sum_send_sem.at[c, source], sum_recv_sem.at[c, source], "dp", source,
            ).wait_recv()
            own = own + sum_recv[c, source].astype(jnp.float32)
        all_send[c] = own.astype(all_send.dtype)
        for k in range(1, m):
            all_copy(c, (mine + k) % m).start()
        grad[:, at, columns(mine)] = own.reshape(27, half, quarter)

    await_hidden(0)
    weight_part(0)

    w2_copy.wait()
    terms[...] = jnp.dot(w2[...], cot[...], preferred_element_type=jnp.float32)

    def term(x, b, c):
        if x % 2 == 0:
            return terms[cell_block(1, b, c, x // 2)]
        value = terms[cell_block(2, b, c, x // 2)]
        if x // 2 + 1 < planes:
            value = value + terms[cell_block(0, b, c, x // 2 + 1)]
        return value

    def back_copy(peer):
        return to_device(
            back_send.at[peer], back_recv.at[me], back_send_sem.at[peer], back_recv_sem.at[me], "space", peer
        )

    for x in range(depth):
        corner = term(x, 0, 2) + moved_back(term(x, 0, 0), False, True, row_len)
        phases = [
            term(x, 1, 1),
            term(x, 1, 2) + moved_back(term(x, 1, 0), False, True, row_len),
            term(x, 2, 1) + moved_back(term(x, 0, 1), True, False, row_len),
            term(x, 2, 2)
            + moved_back(term(x, 2, 0), False, True, row_len)
            + moved_back(corner, True, False, row_len),
        ]
        for phase in range(4):
            back_send[x, :, phase * cells : (phase + 1) * cells] = phases[phase].astype(back_send.dtype)
    for c in range(1, chunks):
        await_hidden(c)
        if c == chunks - 1:
            for k in range(1, n):
                back_copy((me + k) % n).start()
        weight_part(c)
        sum_part(c - 1)
    back_recv[me] = back_send[me]
    sum_part(chunks - 1)

    for k in range(1, n):
        source = (me + k) % n
        to_device(
            back_send.at[source], back_recv.at[source], back_send_sem.at[source], back_recv_sem.at[source], "space", source
        ).wait_recv()
    for g in range(n):
        cut = slice(g * group, (g + 1) * group)
        pre_grad[cut, :] = (back_recv[g].astype(jnp.float32) * slope_of(pre[cut, :])).astype(pre_grad.dtype)
    for c in range(chunks):
        for k in range(1, m):
            source = (mine + k) % m
            to_device(
                all_send.at[c], all_recv.at[c, source],
                all_send_sem.at[c, source], all_recv_sem.at[c, source], "dp", source,
            ).wait_recv()
            grad[:, c * half : (c + 1) * half, columns(source)] = (
                all_recv[c, source].astype(jnp.float32).reshape(27, half, quarter)
            )

    finish = lambda copy: copy.wait_send()
    cot_copy(me, 2).wait_send()
    for h in range(chips - 1):
        cot_send(h, finish)
        cot_pass(h + 1, False, finish)

    @pl.when(me < n - 1)
    def _():
        for c in range(chunks):
            rim_copy(c).wait_send()

    for k in range(1, n):
        back_copy((me + k) % n).wait_send()
    for c in range(chunks):
        for k in range(1, n):
            hid_copy(c, (me + k) % n).wait_send()
        for k in range(1, m):
            sum_copy(c, (mine + k) % m).wait_send()
            all_copy(c, (mine + k) % m).wait_send()


def per_device(volume, w_first, w_second, cotangent):
    n = lax.axis_size("space")
    m = lax.axis_size("dp")
    channels = volume.shape[1]
    cells = volume.shape[4]
    out_channels = w_first.shape[4]
    group = w_second.shape[3]
    last = w_second.shape[4]
    row_len = WID // 4
    if volume.shape[2] != 2 or group % 32 or (last // m) % 128 or n % 2:
        return plain_device(volume, w_first, w_second, cotangent)
    planes = jnp.transpose(volume[0], (1, 2, 0, 3))
    span = 4 * cells
    chunks = 2
    rows = 27 * group
    cot_planes = cotangent.shape[2]
    out_cells = cot_planes * cells
    quarter = last // m
    bf16, f32 = jnp.bfloat16, jnp.float32
    vmem = pl.BlockSpec(memory_space=pltpu.VMEM)
    anywhere = pl.BlockSpec(memory_space=pl.ANY)
    dma = pltpu.SemaphoreType.DMA
    grad, pre_grad = pl.pallas_call(
        functools.partial(section_kernel, n, m, row_len, chunks),
        out_shape=(
            jax.ShapeDtypeStruct((27, group, last), f32),
            jax.ShapeDtypeStruct((out_channels, span), bf16),
        ),
        in_specs=[vmem, anywhere, anywhere, vmem],
        out_specs=(vmem, vmem),
        scratch_shapes=[
            pltpu.VMEM((27 * channels, out_channels), bf16),
            pltpu.VMEM((rows, last), bf16),
            pltpu.VMEM((last, out_cells), bf16),
            pltpu.VMEM((9 * channels, span), bf16),
            pltpu.VMEM((out_channels, span), f32),
            pltpu.VMEM((out_channels, span), bf16),
            pltpu.VMEM((out_channels, span), bf16),
            pltpu.VMEM((chunks, n, group // chunks, span), bf16),
            pltpu.VMEM((chunks, n, group // chunks, span), bf16),
            pltpu.VMEM((rows, out_cells), bf16),
            pltpu.VMEM((rows, out_cells), f32),
            pltpu.VMEM((n, group, span), bf16),
            pltpu.VMEM((n, group, span), bf16),
            pltpu.VMEM((chunks, m, rows // chunks, quarter), bf16),
            pltpu.VMEM((chunks, m, rows // chunks, quarter), bf16),
            pltpu.VMEM((chunks, rows // chunks, quarter), bf16),
            pltpu.VMEM((chunks, m, rows // chunks, quarter), bf16),
            dma((3,)),
            dma((1,)),
            dma((3, n)),
            dma((n,)),
            dma((chunks,)),
            dma((chunks,)),
            dma((chunks, n)),
            dma((chunks, n)),
            dma((n,)),
            dma((n,)),
            dma((chunks, m)),
            dma((chunks, m)),
            dma((chunks, m)),
            dma((chunks, m)),
        ],
        compiler_params=pltpu.CompilerParams(
            collective_id=0, has_side_effects=True, vmem_limit_bytes=50 * 2**20
        ),
        cost_estimate=pl.CostEstimate(
            flops=2 * 27 * channels * out_channels * span + 4 * rows * last * out_cells,
            bytes_accessed=10 * 2**20,
            transcendentals=0,
        ),
    )(
        planes,
        w_first.reshape(27 * channels, out_channels),
        w_second.reshape(rows, last),
        cotangent[0],
    )
    return (
        grad.reshape(3, 3, 3, group, last),
        pre_grad.reshape(1, out_channels, 1, 4, cells),
    )


def solution(mesh):
    in_specs = (
        P("dp", None, "space", None, None),
        P(),
        P(None, None, None, "space", None),
        P("dp", "space", None, None),
    )
    out_specs = (P(None, None, None, "space", None), P("dp", None, "space", None, None))
    return jax.shard_map(
        per_device, mesh=mesh, in_specs=in_specs, out_specs=out_specs, check_vma=False
    )
```

```python
import functools

import jax
import jax.numpy as jnp
from jax import lax
from jax.experimental import pallas as pl
from jax.experimental.pallas import tpu as pltpu
from jax.sharding import PartitionSpec as P

C3 = 512
WID = 128


leak_slope = 0.3


def from_behind(block, axis, distance):
    devices = range(lax.axis_size(axis))
    route = [(i - distance, i) for i in devices if i - distance in devices]
    return lax.ppermute(block, axis, route)


def activate(values):
    return leak_slope * values + (1.0 - leak_slope) * values * jax.nn.sigmoid(values)


def slope_of(values):
    sigmoid_value = jax.nn.sigmoid(values)
    return leak_slope + (1.0 - leak_slope) * (
        sigmoid_value + values * sigmoid_value * (1.0 - sigmoid_value)
    )


def stride_taps(values, along_dim):
    length = values.shape[along_dim] // 2
    paired = values.reshape(values.shape[:along_dim] + (length, 2) + values.shape[along_dim + 1 :])
    even_cells = lax.index_in_dim(paired, 0, along_dim + 1, keepdims=False)
    odd_cells = lax.index_in_dim(paired, 1, along_dim + 1, keepdims=False)
    before = jnp.concatenate(
        [
            jnp.zeros_like(lax.slice_in_dim(odd_cells, 0, 1, axis=along_dim)),
            lax.slice_in_dim(odd_cells, 0, length - 1, axis=along_dim),
        ],
        along_dim,
    )
    return [before, even_cells, odd_cells]


def step_cells(values, by_row, by_col, row_len):
    cells = values.shape[-1]
    if by_row:
        filler = jnp.zeros(values.shape[:-1] + (row_len,), values.dtype)
        values = jnp.concatenate([filler, values[..., : cells - row_len]], -1)
    if by_col:
        filler = jnp.zeros(values.shape[:-1] + (1,), values.dtype)
        moved = jnp.concatenate([filler, values[..., : cells - 1]], -1)
        keeper = lax.iota(jnp.int32, cells) % row_len != 0
        values = jnp.where(keeper, moved, jnp.zeros_like(moved))
    return values


def plane_taps(values, row_len):
    phases = values.shape[-2]
    out_phases = phases // 2
    collected = []
    for row_tap in range(3):
        for col_tap in range(3):
            rows_out = []
            for row_phase in range(out_phases):
                cols_out = []
                for col_phase in range(out_phases):
                    row_at = 2 * row_phase + row_tap - 1
                    col_at = 2 * col_phase + col_tap - 1
                    part = values[..., row_at % phases, col_at % phases, :]
                    cols_out.append(step_cells(part, row_at < 0, col_at < 0, row_len))
                rows_out.append(jnp.stack(cols_out, -2))
            collected.append(jnp.stack(rows_out, -3))
    return collected


def all_taps(values, row_len):
    collected = []
    for depth_part in stride_taps(values, 1):
        collected.extend(plane_taps(depth_part, row_len))
    return collected


def contract_first(left_side, right_side):
    return lax.dot_general(
        left_side, right_side, (((0,), (0,)), ((), ())), preferred_element_type=jnp.float32
    )


def contract_last(left_side, right_side):
    return lax.dot_general(
        left_side, right_side, (((1,), (1,)), ((), ())), preferred_element_type=jnp.float32
    )


def plain_device(volume, w_first, w_second, cotangent):
    channels = volume.shape[1]
    depth_cells = volume.shape[2]
    cell_count = volume.shape[4]
    half_depth = depth_cells // 2
    out_channels = w_first.shape[4]
    row_len = WID // 4
    paired = volume[0].reshape(channels, half_depth, 2, 4, 4, cell_count)
    even_cells = paired[:, :, 0]
    odd_cells = paired[:, :, 1]
    w_flat = w_first.reshape(27 * channels, out_channels)
    rim_cells = from_behind(odd_cells, "space", 1)
    before = jnp.concatenate([rim_cells, odd_cells[:, : half_depth - 1]], 1)
    collected = []
    for depth_part in (before, even_cells, odd_cells):
        collected.extend(plane_taps(depth_part, row_len))
    stacked = jnp.stack(collected, 0).reshape(27 * channels, -1)
    pre_act = contract_first(w_flat, stacked).reshape(out_channels, half_depth, 4, cell_count)
    hidden = activate(pre_act).astype(jnp.bfloat16)
    by_channel = lax.all_to_all(hidden, "space", split_axis=0, concat_axis=1, tiled=True)
    own_channels = by_channel.shape[0]
    full_depth = by_channel.shape[1]
    hidden_cells = by_channel.reshape(own_channels, full_depth, 2, 2, cell_count)
    hidden_taps = jnp.stack(all_taps(hidden_cells, row_len), 0).reshape(27 * own_channels, -1)
    w_rows = w_second.reshape(27 * own_channels, C3)
    out_cells = hidden_taps.shape[1]
    gathered = lax.all_gather(cotangent[0], "space", axis=0, tiled=True)
    cot_flat = gathered.reshape(C3, out_cells)
    weight_grad = contract_last(hidden_taps, cot_flat)
    tap_terms = jnp.dot(w_rows, cot_flat, preferred_element_type=jnp.float32)
    grad_second = lax.psum(weight_grad, "dp").reshape(3, 3, 3, own_channels, C3)

    def spread(field):
        return jnp.stack(all_taps(field, row_len), 0).reshape(27 * own_channels, -1)

    unused, pull = jax.vjp(
        spread, jnp.zeros((own_channels, full_depth, 2, 2, cell_count), jnp.float32)
    )
    back_terms = pull(tap_terms)[0]
    back_terms = back_terms.astype(jnp.bfloat16).reshape(own_channels, full_depth, 4, cell_count)
    hidden_grad = lax.all_to_all(back_terms, "space", split_axis=1, concat_axis=0, tiled=True)
    pre_grad = (hidden_grad.astype(jnp.float32) * slope_of(pre_act)).astype(jnp.bfloat16)
    return (grad_second, pre_grad[None])


def moved_cells(block, by_row, by_col, row_len):
    if not (by_row or by_col):
        return block
    cells = block.shape[-1]
    at = lax.broadcasted_iota(jnp.int32, block.shape, 1)
    wide = block.astype(jnp.float32)
    if by_row:
        wide = jnp.where(at >= row_len, pltpu.roll(wide, row_len, 1), 0.0)
    if by_col:
        wide = jnp.where(at % row_len != 0, pltpu.roll(wide, 1, 1), 0.0)
    return wide.astype(block.dtype)


def moved_back(block, by_row, by_col, row_len):
    cells = block.shape[-1]
    at = lax.broadcasted_iota(jnp.int32, block.shape, 1)
    if by_row:
        block = pltpu.roll(jnp.where(at >= row_len, block, 0.0), cells - row_len, 1)
    if by_col:
        block = pltpu.roll(jnp.where(at % row_len != 0, block, 0.0), cells - 1, 1)
    return block


def fill_taps(plane, taps, row_len):
    _, channels, cells = plane.shape
    for row_tap in range(3):
        for col_tap in range(3):
            top = (row_tap * 3 + col_tap) * channels
            for row_phase in range(2):
                for col_phase in range(2):
                    row_at = 2 * row_phase + row_tap - 1
                    col_at = 2 * col_phase + col_tap - 1
                    part = plane[(row_at % 4) * 4 + col_at % 4]
                    left = (row_phase * 2 + col_phase) * cells
                    taps[top : top + channels, left : left + cells] = moved_cells(
                        part, row_at < 0, col_at < 0, row_len
                    )


def greet(axes):
    barrier = pltpu.get_barrier_semaphore()
    for axis, size in axes:
        me = lax.axis_index(axis)
        for k in range(1, size):
            pl.semaphore_signal(
                barrier, inc=1, device_id={axis: (me + k) % size}, device_id_type=pl.DeviceIdType.MESH
            )


def await_greetings(axes):
    pl.semaphore_wait(pltpu.get_barrier_semaphore(), sum(size - 1 for _, size in axes))


def to_device(src, dst, send_sem, recv_sem, axis, peer):
    return pltpu.make_async_remote_copy(
        src_ref=src,
        dst_ref=dst,
        send_sem=send_sem,
        recv_sem=recv_sem,
        device_id={axis: peer},
        device_id_type=pl.DeviceIdType.MESH,
    )


def section_kernel(
    n, m, row_len, chunks,
    vol, w1_hbm, w2_hbm, cot_own, grad, pre_grad,
    w1, w2, cot, taps, pre, part, rim, hid_send, hid_recv,
    out_taps, terms, back_send, back_recv, sum_send, sum_recv, all_send, all_recv,
    w1_sem, w2_sem, cot_send_sem, cot_recv_sem, rim_send_sem, rim_recv_sem, hid_send_sem, hid_recv_sem,
    back_send_sem, back_recv_sem, sum_send_sem, sum_recv_sem, all_send_sem, all_recv_sem,
):
    me = lax.axis_index("space")
    mine = lax.axis_index("dp")
    chips = n // 2
    chip = me // 2
    core = me % 2
    channels = vol.shape[2]
    cells = vol.shape[3]
    rows = 9 * channels
    out_channels = w1.shape[1]
    wide = out_channels // chunks
    group = out_channels // n
    half = group // chunks
    tap_rows = 27 * half
    depth = n
    planes = depth // 2
    quarter = cot.shape[0] // m
    share = cot_own.shape[0]

    def w1_copy(a):
        cut = pl.ds(a * rows, rows)
        return pltpu.make_async_copy(w1_hbm.at[cut], w1.at[cut], w1_sem.at[a])

    axes = [("space", n), ("dp", m)]
    greet(axes)
    for a in (0, 2, 1):
        w1_copy(a).start()
    w2_copy = pltpu.make_async_copy(w2_hbm, w2, w2_sem.at[0])
    w2_copy.start()
    own_rows = pl.ds(pl.multiple_of(me * share, share), share)
    for s in range(planes):
        cot[own_rows, s * cells : (s + 1) * cells] = cot_own[:, s, :]
    fill_taps(vol.at[1], taps, row_len)
    await_greetings(axes)

    def cot_copy(block, way):
        cut = pl.ds(pl.multiple_of(block * share, share), share)
        peer = [(me + 2) % n, (me + n - 2) % n, 2 * chip + 1 - core][way]
        return to_device(
            cot.at[cut], cot.at[cut], cot_send_sem.at[way, block], cot_recv_sem.at[block], "space", peer
        )

    def cot_send(h, act):
        up = 2 * ((chip - h + chips) % chips) + core
        down = 2 * ((chip + h) % chips) + core

        @pl.when((chip - h >= 0) & (chip + 1 < chips))
        def _():
            act(cot_copy(up, 0))

        @pl.when((chip + h < chips) & (chip - 1 >= 0))
        def _():
            act(cot_copy(down, 1))

    def cot_pass(h, wait, act):
        up = 2 * ((chip - h + chips) % chips) + core
        down = 2 * ((chip + h) % chips) + core

        @pl.when(chip - h >= 0)
        def _():
            if wait:
                cot_copy(up, 2).wait_recv()
            act(cot_copy(up, 2))

        @pl.when(chip + h < chips)
        def _():
            if wait:
                cot_copy(down, 2).wait_recv()
            act(cot_copy(down, 2))

    start = lambda copy: copy.start()
    cot_copy(me, 2).start()
    cot_send(0, start)

    w1_copy(0).wait()

    def rim_copy(c):
        cut = pl.ds(c * wide, wide)
        return to_device(
            part.at[cut], rim.at[cut], rim_send_sem.at[c], rim_recv_sem.at[c], "space", (me + 1) % n
        )

    before = contract_first(w1[0:rows, :], taps[...])
    for c in range(chunks):
        for g in range(n):
            from_row = g * group + c * half
            to_row = c * wide + g * half
            part[to_row : to_row + half, :] = before[from_row : from_row + half].astype(part.dtype)

        @pl.when(me < n - 1)
        def _():
            rim_copy(c).start()

    w1_copy(2).wait()
    pre[...] = contract_first(w1[2 * rows : 3 * rows, :], taps[...])
    fill_taps(vol.at[0], taps, row_len)
    w1_copy(1).wait()
    pre[...] += contract_first(w1[rows : 2 * rows, :], taps[...])

    cot_pass(1, True, start)
    cot_send(1, start)

    def hid_copy(c, peer):
        return to_device(
            hid_send.at[c, peer], hid_recv.at[c, me], hid_send_sem.at[c, peer], hid_recv_sem.at[c, me], "space", peer
        )

    for c in range(chunks):

        @pl.when(me > 0)
        def _():
            rim_copy(c).wait_recv()
            for g in range(n):
                to_row = g * group + c * half
                from_row = c * wide + g * half
                pre[to_row : to_row + half, :] += rim[from_row : from_row + half, :].astype(jnp.float32)

        for g in range(n):
            at = g * group + c * half
            hid_send[c, g] = activate(pre[at : at + half, :]).astype(hid_send.dtype)
        for k in range(1, n):
            hid_copy(c, (me + k) % n).start()

    for h in range(2, chips):
        cot_pass(h, True, start)
        if h + 1 < chips:
            cot_send(h, start)
    for c in range(chunks):
        hid_recv[c, me] = hid_send[c, me]
    for z in range(chips):
        cot_copy(2 * z + 1 - core, 2).wait_recv()

    def cell_block(a, b, c, s):
        top = ((a * 3 + b) * 3 + c) * group
        return (slice(top, top + group), slice(s * cells, (s + 1) * cells))

    def sum_copy(c, peer):
        return to_device(
            sum_send.at[c, peer], sum_recv.at[c, mine], sum_send_sem.at[c, peer], sum_recv_sem.at[c, mine], "dp", peer
        )

    def all_copy(c, peer):
        return to_device(
            all_send.at[c], all_recv.at[c, mine], all_send_sem.at[c, peer], all_recv_sem.at[c, mine], "dp", peer
        )

    def columns(owner):
        return pl.ds(pl.multiple_of(owner * quarter, quarter), quarter)

    def await_hidden(c):
        for k in range(1, n):
            source = (me + k) % n
            to_device(
                hid_send.at[c, source], hid_recv.at[c, source],
                hid_send_sem.at[c, source], hid_recv_sem.at[c, source], "space", source,
            ).wait_recv()

    def weight_part(c):
        def tap_block(a, b, e, s):
            top = c * tap_rows + ((a * 3 + b) * 3 + e) * half
            return (slice(top, top + half), slice(s * cells, (s + 1) * cells))

        for x in range(depth):
            for b in range(3):
                for e in range(3):
                    phase = 2 * ((b + 1) % 2) + (e + 1) % 2
                    value = moved_cells(
                        hid_recv[c, x, :, phase * cells : (phase + 1) * cells], b == 0, e == 0, row_len
                    )
                    if x % 2 == 0:
                        out_taps[tap_block(1, b, e, x // 2)] = value
                    else:
                        out_taps[tap_block(2, b, e, x // 2)] = value
                        if x // 2 + 1 < planes:
                            out_taps[tap_block(0, b, e, x // 2 + 1)] = value
                    if x == 0:
                        out_taps[tap_block(0, b, e, 0)] = jnp.zeros_like(value)
        mine_taps = slice(c * tap_rows, (c + 1) * tap_rows)
        for k in range(1, m):
            peer = (mine + k) % m
            sum_send[c, peer] = contract_last(out_taps[mine_taps, :], cot[columns(peer), :]).astype(sum_send.dtype)
            sum_copy(c, peer).start()
        own = contract_last(out_taps[mine_taps, :], cot[columns(mine), :])
        grad[:, c * half : (c + 1) * half, columns(mine)] = own.reshape(27, half, quarter)

    def sum_part(c):
        at = slice(c * half, (c + 1) * half)
        own = grad[:, at, columns(mine)].reshape(tap_rows, quarter)
        for k in range(1, m):
            source = (mine + k) % m
            to_device(
                sum_send.at[c, source], sum_recv.at[c, source],
                sum_send_sem.at[c, source], sum_recv_sem.at[c, source], "dp", source,
            ).wait_recv()
            own = own + sum_recv[c, source].astype(jnp.float32)
        all_send[c] = own.astype(all_send.dtype)
        for k in range(1, m):
            all_copy(c, (mine + k) % m).start()
        grad[:, at, columns(mine)] = own.reshape(27, half, quarter)

    await_hidden(0)
    weight_part(0)

    w2_copy.wait()
    terms[...] = jnp.dot(w2[...], cot[...], preferred_element_type=jnp.float32)

    def term(x, b, c):
        if x % 2 == 0:
            return terms[cell_block(1, b, c, x // 2)]
        value = terms[cell_block(2, b, c, x // 2)]
        if x // 2 + 1 < planes:
            value = value + terms[cell_block(0, b, c, x // 2 + 1)]
        return value

    def back_copy(peer):
        return to_device(
            back_send.at[peer], back_recv.at[me], back_send_sem.at[peer], back_recv_sem.at[me], "space", peer
        )

    for x in range(depth):
        corner = term(x, 0, 2) + moved_back(term(x, 0, 0), False, True, row_len)
        phases = [
            term(x, 1, 1),
            term(x, 1, 2) + moved_back(term(x, 1, 0), False, True, row_len),
            term(x, 2, 1) + moved_back(term(x, 0, 1), True, False, row_len),
            term(x, 2, 2)
            + moved_back(term(x, 2, 0), False, True, row_len)
            + moved_back(corner, True, False, row_len),
        ]
        for phase in range(4):
            back_send[x, :, phase * cells : (phase + 1) * cells] = phases[phase].astype(back_send.dtype)
    for c in range(1, chunks):
        await_hidden(c)
        if c == chunks - 1:
            for k in range(1, n):
                back_copy((me + k) % n).start()
        weight_part(c)
        sum_part(c - 1)
    back_recv[me] = back_send[me]
    sum_part(chunks - 1)

    for k in range(1, n):
        source = (me + k) % n
        to_device(
            back_send.at[source], back_recv.at[source], back_send_sem.at[source], back_recv_sem.at[source], "space", source
        ).wait_recv()
    for g in range(n):
        cut = slice(g * group, (g + 1) * group)
        pre_grad[cut, :] = (back_recv[g].astype(jnp.float32) * slope_of(pre[cut, :])).astype(pre_grad.dtype)
    for c in range(chunks):
        for k in range(1, m):
            source = (mine + k) % m
            to_device(
                all_send.at[c], all_recv.at[c, source],
                all_send_sem.at[c, source], all_recv_sem.at[c, source], "dp", source,
            ).wait_recv()
            grad[:, c * half : (c + 1) * half, columns(source)] = (
                all_recv[c, source].astype(jnp.float32).reshape(27, half, quarter)
            )

    finish = lambda copy: copy.wait_send()
    cot_copy(me, 2).wait_send()
    for h in range(chips - 1):
        cot_send(h, finish)
        cot_pass(h + 1, False, finish)

    @pl.when(me < n - 1)
    def _():
        for c in range(chunks):
            rim_copy(c).wait_send()

    for k in range(1, n):
        back_copy((me + k) % n).wait_send()
    for c in range(chunks):
        for k in range(1, n):
            hid_copy(c, (me + k) % n).wait_send()
        for k in range(1, m):
            sum_copy(c, (mine + k) % m).wait_send()
            all_copy(c, (mine + k) % m).wait_send()


def per_device(volume, w_first, w_second, cotangent):
    n = lax.axis_size("space")
    m = lax.axis_size("dp")
    channels = volume.shape[1]
    cells = volume.shape[4]
    out_channels = w_first.shape[4]
    group = w_second.shape[3]
    last = w_second.shape[4]
    row_len = WID // 4
    if volume.shape[2] != 2 or group % 32 or (last // m) % 128 or n % 2:
        return plain_device(volume, w_first, w_second, cotangent)
    planes = jnp.transpose(volume[0], (1, 2, 0, 3))
    span = 4 * cells
    chunks = 2
    rows = 27 * group
    cot_planes = cotangent.shape[2]
    out_cells = cot_planes * cells
    quarter = last // m
    bf16, f32 = jnp.bfloat16, jnp.float32
    vmem = pl.BlockSpec(memory_space=pltpu.VMEM)
    anywhere = pl.BlockSpec(memory_space=pl.ANY)
    dma = pltpu.SemaphoreType.DMA
    grad, pre_grad = pl.pallas_call(
        functools.partial(section_kernel, n, m, row_len, chunks),
        out_shape=(
            jax.ShapeDtypeStruct((27, group, last), f32),
            jax.ShapeDtypeStruct((out_channels, span), bf16),
        ),
        in_specs=[vmem, anywhere, anywhere, vmem],
        out_specs=(vmem, vmem),
        scratch_shapes=[
            pltpu.VMEM((27 * channels, out_channels), bf16),
            pltpu.VMEM((rows, last), bf16),
            pltpu.VMEM((last, out_cells), bf16),
            pltpu.VMEM((9 * channels, span), bf16),
            pltpu.VMEM((out_channels, span), f32),
            pltpu.VMEM((out_channels, span), bf16),
            pltpu.VMEM((out_channels, span), bf16),
            pltpu.VMEM((chunks, n, group // chunks, span), bf16),
            pltpu.VMEM((chunks, n, group // chunks, span), bf16),
            pltpu.VMEM((rows, out_cells), bf16),
            pltpu.VMEM((rows, out_cells), f32),
            pltpu.VMEM((n, group, span), bf16),
            pltpu.VMEM((n, group, span), bf16),
            pltpu.VMEM((chunks, m, rows // chunks, quarter), bf16),
            pltpu.VMEM((chunks, m, rows // chunks, quarter), bf16),
            pltpu.VMEM((chunks, rows // chunks, quarter), bf16),
            pltpu.VMEM((chunks, m, rows // chunks, quarter), bf16),
            dma((3,)),
            dma((1,)),
            dma((3, n)),
            dma((n,)),
            dma((chunks,)),
            dma((chunks,)),
            dma((chunks, n)),
            dma((chunks, n)),
            dma((n,)),
            dma((n,)),
            dma((chunks, m)),
            dma((chunks, m)),
            dma((chunks, m)),
            dma((chunks, m)),
        ],
        compiler_params=pltpu.CompilerParams(
            collective_id=0, has_side_effects=True, vmem_limit_bytes=32 * 2**20
        ),
        cost_estimate=pl.CostEstimate(
            flops=2 * 27 * channels * out_channels * span + 4 * rows * last * out_cells,
            bytes_accessed=10 * 2**20,
            transcendentals=0,
        ),
    )(
        planes,
        w_first.reshape(27 * channels, out_channels),
        w_second.reshape(rows, last),
        cotangent[0],
    )
    return (
        grad.reshape(3, 3, 3, group, last),
        pre_grad.reshape(1, out_channels, 1, 4, cells),
    )


def solution(mesh):
    in_specs = (
        P("dp", None, "space", None, None),
        P(),
        P(None, None, None, "space", None),
        P("dp", "space", None, None),
    )
    out_specs = (P(None, None, None, "space", None), P("dp", None, "space", None, None))
    return jax.shard_map(
        per_device, mesh=mesh, in_specs=in_specs, out_specs=out_specs, check_vma=False
    )
```
